768 devices in a mesh: dp: 4 (over x), seq: 96 (over z, y), tensor: 2 (over core).
Axes of the slice: x: 4, y: 8, z: 12, core: 2. Of those that a mesh axis runs over, the one named last changes fastest.
Arguments:
- hidden: bfloat16 [4, 49152, 4096], P('dp', ('seq', 'tensor')), may hold values from -6 to 6
- lengths: int32 [4, 12], replicated, may hold values from 1 to 12288, 49152 in all within a row
- positive: int32 [48], replicated, may hold values from 0 to 47, as said below
- gain: float32 [4096], replicated, may hold values from 0.5 to 1.5
Outputs:
- hidden_grad: bfloat16 [4, 49152, 4096], P('dp', ('seq', 'tensor'))
- loss: float32 [], replicated
The draws below stay inside these ranges and needn't reach their ends.
Inputs may be any that keep to these rules, and one draw needn't show every extreme that they name: Each sequence's 12 lengths sum to 49152. positive[i] != i and positive[positive[i]] = i.
All inputs are finite; a program needn't handle non-finite values.
Results may differ from the reference program's by a relative error of at most 0.002.
Values sent between devices are 32-bit elements; how exact they have to be, the bound alone decides.
No kernel may reach another device: no remote copies, remote signals or barrier semaphores. Data moves between devices by JAX's collectives and lax.ppermute only.
A program may use at most 32 MiB of HBM per device.

```python
import math
import jax
import jax.numpy as jnp
import numpy as np
from jax import lax

D = 4096
DOCS = 12
TOK_DEV = 256
LENGTH = 49152
BATCH_DOCS = 48
MOST_LEN = 12288
N_DP = 4
N_SEQ = 96
N_TENSOR = 2


def draw_positive(key, part):
    key = jax.random.fold_in(key, 7)
    order = jax.random.permutation(key, BATCH_DOCS).astype(jnp.int32)
    partner = order.reshape(-1, 2)[:, ::-1].reshape(-1)
    return jnp.zeros((BATCH_DOCS,), jnp.int32).at[order].set(partner)


def levels(rng, dims, pieces, least, largest):
    factor_of, own = 1.0, jax.random.fold_in(rng, 6)
    for axis_at, shards_of in pieces:
        steps = jnp.exp(jax.random.uniform(jax.random.fold_in(own, axis_at), (shards_of,), jnp.float32, least / len(pieces), largest / len(pieces)))
        factor_of = factor_of * jnp.repeat(steps, dims[axis_at] // shards_of).reshape([-1 if axis == axis_at else 1 for axis in range(len(dims))])
    return factor_of


def split_up(number_of, total, reach, slope):
    portions = [(1 << 20) // math.isqrt(grade ** slope) + 1 for grade in range(2, number_of + 1)]
    spare, counts = total - reach - (number_of - 1), [1] * (number_of - 1)
    while spare > 0:
        candidates = [i for i in range(number_of - 1) if counts[i] < reach]
        pool, left = sum([portions[i] for i in candidates]), spare
        for i in candidates:
            addition = min(reach - counts[i], max(1, left * portions[i] // pool), spare)
            counts[i] = counts[i] + addition
            spare = spare - addition
    return np.array([reach] + counts)


def ragged_sizes(own_key, amount, total, bound, skew):
    if amount == 2:
        one = jax.random.randint(own_key, (), max(1, total - bound), min(bound, total - 1) + 1)
        return jnp.stack([one, total - one])
    tallies = jnp.asarray(split_up(amount, total, bound, skew), jnp.int32)
    twos = (amount - 1) // 2
    source_of, taker = tallies[1:1 + 2 * twos:2], tallies[2:2 + 2 * twos:2]
    room = jnp.minimum(source_of - 1, bound - taker)
    passed = jax.random.randint(jax.random.fold_in(own_key, 1), (twos,), 0, 1 << 20) % (room + 1)
    tallies = tallies.at[1:1 + 2 * twos:2].set(source_of - passed).at[2:2 + 2 * twos:2].set(taker + passed)
    return tallies[jax.random.permutation(jax.random.fold_in(own_key, 2), amount)]


def normal_values(stream_key, extent, spread, limit, split=(), held_as=jnp.bfloat16):
    entries = spread * jax.random.normal(stream_key, extent, jnp.float32)
    if split:
        entries = entries * levels(stream_key, extent, split, -0.22, 0.18)
    return jnp.clip(entries, -limit, limit).astype(held_as)


def setup_inputs(seed: int = 0) -> dict:
    seeds = jax.random.split(jax.random.key(seed), 5)
    hidden = normal_values(seeds[0], (N_DP, LENGTH, D), 1.0, 6.0, ((0, 4), (1, 192)))
    lengths = jax.vmap(lambda own: ragged_sizes(own, DOCS, LENGTH, MOST_LEN, 2))(jax.random.split(seeds[1], N_DP)).reshape((N_DP, DOCS)).astype(jnp.int32)
    positive = draw_positive(jax.random.fold_in(seeds[4], 71), 0)
    gain = jnp.clip(1.0 + 0.1 * jax.random.normal(seeds[3], (D,), jnp.float32), 0.5, 1.5)
    return dict(hidden=hidden, lengths=lengths, positive=positive, gain=gain)


tau_value = 0.05
loss_factor = 65536.0
norm_eps = 1e-06
embed_eps = 1e-12

def membership(lens, positions):
    ends = jnp.cumsum(lens)
    starts = ends - lens
    inside = (positions[None, :] >= starts[:, None]) & (positions[None, :] < ends[:, None])
    return inside.astype(jnp.float32)

def contrast(means, positive):
    square = lax.optimization_barrier(jnp.sum(means * means, axis=1))
    inverse = 1.0 / jnp.sqrt(square + embed_eps)
    unit = means * inverse[:, None]
    scores = jnp.dot(unit, unit.T, precision=lax.Precision.HIGHEST) / tau_value
    count = means.shape[0]
    ident = lax.iota(jnp.int32, count)
    offdiag = (ident[:, None] != ident[None, :]).astype(jnp.float32)
    weights = jnp.exp(scores) * offdiag
    totals = lax.optimization_barrier(jnp.sum(weights, axis=1))
    picked = (ident[None, :] == positive[:, None]).astype(jnp.float32)
    loss = jnp.sum(jnp.log(totals) - lax.optimization_barrier(jnp.sum(scores * picked, axis=1)))
    grad_scores = weights / totals[:, None] - picked
    grad_unit = jnp.dot(grad_scores + grad_scores.T, unit, precision=lax.Precision.HIGHEST) / tau_value
    along = lax.optimization_barrier(jnp.sum(means * grad_unit, axis=1))
    grad_means = grad_unit * inverse[:, None] - means * (inverse ** 3 * along)[:, None]
    return (loss, grad_means)

def reference(hidden, lengths, positive, gain):
    block = TOK_DEV * N_TENSOR
    numbers = jnp.arange(N_SEQ, dtype=jnp.int32)

    def pool_group(items):
        rows_all, lens = items
        blocks = rows_all.reshape(N_SEQ, block, D)

        def step(total, item):
            rows, number = item
            values = rows.astype(jnp.float32)
            scale = lax.rsqrt(lax.optimization_barrier(jnp.mean(values * values, axis=1)) + norm_eps)
            positions = number * block + lax.iota(jnp.int32, block)
            weights = membership(lens, positions) * scale[None, :]
            return (total + jnp.dot(weights, values, precision=lax.Precision.HIGHEST), None)
        total, _ = lax.scan(step, jnp.zeros((DOCS, D), jnp.float32), (blocks, numbers))
        return total
    sums = lax.map(pool_group, (hidden, lengths))
    means = (sums * gain[None, None, :] / lengths.astype(jnp.float32)[:, :, None]).reshape(BATCH_DOCS, D)
    loss, grad_means = contrast(means, positive)
    grad_means = grad_means.reshape(N_DP, DOCS, D)

    def grad_group(items):
        rows_all, lens, grads = items
        per_doc = grads / lens.astype(jnp.float32)[:, None]
        blocks = rows_all.reshape(N_SEQ, block, D)

        def step(carry, item):
            rows, number = item
            values = rows.astype(jnp.float32)
            scale = lax.rsqrt(lax.optimization_barrier(jnp.mean(values * values, axis=1)) + norm_eps)
            positions = number * block + lax.iota(jnp.int32, block)
            member = membership(lens, positions)
            grad_y = jnp.dot(member.T, per_doc, precision=lax.Precision.HIGHEST)
            weighted = grad_y * gain[None, :]
            inner = lax.optimization_barrier(jnp.sum(weighted * values, axis=1))
            grad_rows = loss_factor * (weighted * scale[:, None] - values * (scale ** 3 * inner / D)[:, None])
            return (carry, grad_rows.astype(jnp.bfloat16))
        _, out = lax.scan(step, jnp.zeros((), jnp.float32), (blocks, numbers))
        return out.reshape(LENGTH, D)
    hidden_grad = lax.map(grad_group, (hidden, lengths, grad_means))
    return (hidden_grad, loss)
```

```python
import functools

import jax
import jax.numpy as jnp
from jax import lax
from jax.experimental import pallas as pl
from jax.experimental.pallas import tpu as pltpu
from jax.sharding import Mesh
from jax.sharding import PartitionSpec as P

tau_value = 0.05
loss_factor = 65536.0
norm_eps = 1e-06
embed_eps = 1e-12

LANES = 128
DOC_ROWS = 16
HIGHEST = lax.Precision.HIGHEST


def doc_bounds(lens_ref, group, docs, shape):
    doc = lax.broadcasted_iota(jnp.int32, shape, 1) % DOC_ROWS
    starts = jnp.zeros(shape, jnp.int32)
    ends = jnp.zeros(shape, jnp.int32)
    total = jnp.int32(0)
    for d in range(docs):
        size = lens_ref[group, d]
        starts = jnp.where(doc == d, total, starts)
        total = total + size
        ends = jnp.where(doc == d, total, ends)
    return starts, ends


def one_hot(lens_ref, group, first, docs, tok):
    starts, ends = doc_bounds(lens_ref, group, docs, (1, LANES))
    positions = first + lax.broadcasted_iota(jnp.int32, (tok, LANES), 0)
    inside = (positions >= starts) & (positions < ends)
    return jnp.where(inside, 1.0, 0.0)


def halves(x):
    high = x.astype(jnp.bfloat16)
    low = (x - high.astype(jnp.float32)).astype(jnp.bfloat16)
    return high, low


def row_scale(values):
    width = values.shape[1]
    return lax.rsqrt(jnp.sum(values * values, axis=1, keepdims=True) * (1.0 / width) + norm_eps)


def shard_number(sizes):
    _, _, n_y, n_t = sizes
    return (lax.axis_index("z") * n_y + lax.axis_index("y")) * n_t + lax.axis_index("t")


def pool_kernel(sizes, lens_ref, rows_ref, out_ref):
    docs = lens_ref.shape[1]
    tok, width = rows_ref.shape
    blocks = out_ref.shape[0]
    columns = width // blocks // LANES
    scale = row_scale(rows_ref[...].astype(jnp.float32))
    member = one_hot(lens_ref, lax.axis_index("dp"), shard_number(sizes) * tok, docs, tok)
    high, low = halves(member * scale)
    lane = lax.broadcasted_iota(jnp.int32, (tok, LANES), 1)
    weights = jnp.where(lane < DOC_ROWS, high.astype(jnp.float32), low.astype(jnp.float32))
    weights = weights.astype(jnp.bfloat16)
    for block in range(blocks):
        cut = width // blocks
        part = lax.dot_general(
            weights, rows_ref[:, block * cut : (block + 1) * cut],
            (((0,), (0,)), ((), ())), preferred_element_type=jnp.float32,
        )
        both = part[:docs] + part[DOC_ROWS : DOC_ROWS + docs]
        for column in range(columns):
            out_ref[block, column * docs : (column + 1) * docs, :] = both[
                :, column * LANES : (column + 1) * LANES
            ]


def sum_kernel(parts_ref, out_ref):
    total = parts_ref[0]
    for k in range(1, parts_ref.shape[0]):
        total = total + parts_ref[k]
    for k in range(out_ref.shape[0]):
        out_ref[k] = total


def contrast(means, lens_ref, positive_ref, group, docs):
    count = means.shape[0]
    gram = lax.dot_general(
        means, means, (((1,), (1,)), ((), ())), precision=HIGHEST, preferred_element_type=jnp.float32
    )
    row = lax.broadcasted_iota(jnp.int32, (count, count), 0)
    col = lax.broadcasted_iota(jnp.int32, (count, count), 1)
    diagonal = jnp.where(row == col, gram, 0.0)
    inv_col = 1.0 / jnp.sqrt(jnp.sum(diagonal, axis=1, keepdims=True) + embed_eps)
    inv_row = 1.0 / jnp.sqrt(jnp.sum(diagonal, axis=0, keepdims=True) + embed_eps)
    scores = gram * inv_col * inv_row * (1.0 / tau_value)
    weights = jnp.where(row == col, 0.0, jnp.exp(scores))
    totals_col = jnp.sum(weights, axis=1, keepdims=True)
    totals_row = jnp.sum(weights, axis=0, keepdims=True)
    picked = jnp.where(positive_ref[...] == row, 1.0, 0.0)
    loss = jnp.sum(jnp.log(totals_row), axis=1, keepdims=True) - jnp.sum(
        jnp.sum(scores * picked, axis=0, keepdims=True), axis=1, keepdims=True
    )
    both = weights / totals_col + weights / totals_row - 2.0 * picked
    along = jnp.sum(both * scores, axis=1, keepdims=True)
    mix = both * (inv_col * inv_row * (1.0 / tau_value))
    mix = mix - jnp.where(row == col, inv_col * inv_col * along, 0.0)
    doc = lax.broadcasted_iota(jnp.int32, (DOC_ROWS, count), 0)
    other = lax.broadcasted_iota(jnp.int32, (DOC_ROWS, count), 1)
    own = jnp.where((other == doc + group * docs) & (doc < docs), 1.0, 0.0)
    size = jnp.ones((DOC_ROWS, 1), jnp.float32)
    at = lax.broadcasted_iota(jnp.int32, (DOC_ROWS, 1), 0)
    for d in range(docs):
        size = jnp.where(at == d, lens_ref[group, d].astype(jnp.float32), size)
    own_mix = jnp.dot(own, mix, precision=HIGHEST, preferred_element_type=jnp.float32)
    return loss, own_mix * (loss_factor / size)


def grad_kernel(sizes, lens_ref, positive_ref, gain_ref, sums_ref, rows_ref, out_ref, loss_ref, means_ref, grads_ref):
    n_dp, _, n_y, n_t = sizes
    docs = lens_ref.shape[1]
    tok, width = rows_ref.shape
    group = lax.axis_index("dp")
    step = pl.program_id(0)
    columns = width // (n_y * n_t) // LANES

    @pl.when(step == 0)
    def _():
        for t in range(n_t):
            for g in range(n_dp):
                for y in range(n_y):
                    for column in range(columns):
                        start = ((y * n_t + t) * columns + column) * LANES
                        means_ref[g * docs : (g + 1) * docs, start : start + LANES] = sums_ref[
                            t, g * n_y + y, column * docs : (column + 1) * docs, :
                        ]
        at = lax.broadcasted_iota(jnp.int32, (n_dp * docs, 1), 0)
        size = jnp.ones((n_dp * docs, 1), jnp.float32)
        for g in range(n_dp):
            for d in range(docs):
                size = jnp.where(at == g * docs + d, lens_ref[g, d].astype(jnp.float32), size)
        means = means_ref[...] * gain_ref[...] * (1.0 / size)
        loss, mix = contrast(means, lens_ref, positive_ref, group, docs)
        loss_ref[...] = loss
        grads = jnp.dot(mix, means, precision=HIGHEST, preferred_element_type=jnp.float32)
        high, low = halves(grads * gain_ref[...])
        grads_ref[:DOC_ROWS] = high
        grads_ref[DOC_ROWS:] = low

    values = rows_ref[...].astype(jnp.float32)
    scale = row_scale(values)
    first = (shard_number(sizes) * pl.num_programs(0) + step) * tok
    member = one_hot(lens_ref, group, first, docs, tok)[:, : 2 * DOC_ROWS].astype(jnp.bfloat16)
    weighted = jnp.dot(member, grads_ref[...], preferred_element_type=jnp.float32)
    inner = jnp.sum(weighted * values, axis=1, keepdims=True)
    out = weighted * scale - values * (scale * scale * scale * inner * (1.0 / width))
    out_ref[...] = out.astype(jnp.bfloat16)


def shards(sizes, hidden, lengths, positive, gain):
    n_dp, n_z, n_y, n_t = sizes
    rows = hidden[0]
    tok, width = rows.shape
    docs = lengths.shape[1]
    blocks = n_y * n_t
    lines = docs * width // blocks // LANES
    smem = pl.BlockSpec(memory_space=pltpu.SMEM)
    vmem = pl.BlockSpec(memory_space=pltpu.VMEM)
    params = pltpu.CompilerParams(vmem_limit_bytes=40 * 2**20)

    def summed(parts, copies):
        return pl.pallas_call(
            sum_kernel,
            out_shape=jax.ShapeDtypeStruct((copies, lines, LANES), jnp.float32),
            in_specs=[vmem], out_specs=vmem, compiler_params=params,
        )(parts)

    share = pl.pallas_call(
        functools.partial(pool_kernel, sizes),
        out_shape=jax.ShapeDtypeStruct((blocks, lines, LANES), jnp.float32),
        in_specs=[smem, vmem], out_specs=vmem, compiler_params=params,
    )(lengths, rows)
    parts = lax.all_to_all(share, ("y", "t"), 0, 0, tiled=True)
    parts = lax.all_to_all(summed(parts, n_z), "z", 0, 0, tiled=True)
    parts = lax.all_to_all(summed(parts, n_dp * n_y), ("dp", "y"), 0, 0, tiled=True)
    sums = lax.all_gather(parts, "t", axis=0)

    steps = 4
    whole = lambda *dims: pl.BlockSpec(dims, lambda i: (0,) * len(dims))
    grads, loss = pl.pallas_call(
        functools.partial(grad_kernel, sizes),
        grid=(steps,),
        out_shape=(
            jax.ShapeDtypeStruct((tok, width), jnp.bfloat16),
            jax.ShapeDtypeStruct((1, 1), jnp.float32),
        ),
        in_specs=[
            smem,
            whole(1, n_dp * docs),
            whole(1, width),
            whole(*sums.shape),
            pl.BlockSpec((tok // steps, width), lambda i: (i, 0)),
        ],
        out_specs=(pl.BlockSpec((tok // steps, width), lambda i: (i, 0)), whole(1, 1)),
        scratch_shapes=[
            pltpu.VMEM((n_dp * docs, width), jnp.float32),
            pltpu.VMEM((2 * DOC_ROWS, width), jnp.bfloat16),
        ],
        compiler_params=params,
    )(lengths, positive.reshape(1, -1), gain.reshape(1, -1), sums, rows)
    return grads[None], loss.reshape(())


def solution(mesh):
    n_dp, n_seq, n_t = mesh.devices.shape
    n_y = 8 if n_seq % 8 == 0 else 2
    sizes = (n_dp, n_seq // n_y, n_y, n_t)
    inner = Mesh(mesh.devices.reshape(sizes), ("dp", "z", "y", "t"))
    split = P("dp", ("z", "y", "t"), None)
    return jax.shard_map(
        functools.partial(shards, sizes),
        mesh=inner,
        in_specs=(split, P(), P(), P()),
        out_specs=(split, P()),
        check_vma=False,
    )
```

```python
import functools

import jax
import jax.numpy as jnp
from jax import lax
from jax.experimental import pallas as pl
from jax.experimental.pallas import tpu as pltpu
from jax.sharding import Mesh
from jax.sharding import PartitionSpec as P

tau_value = 0.05
loss_factor = 65536.0
norm_eps = 1e-06
embed_eps = 1e-12

LANES = 128
DOC_ROWS = 16
CHUNKS = 8
STEPS = 4
Z_ORDER = tuple(range(11, -1, -1))
HIGHEST = lax.Precision.HIGHEST


def one_hot(lens_ref, group, first, docs, tok):
    doc = lax.broadcasted_iota(jnp.int32, (1, LANES), 1) % DOC_ROWS
    starts = jnp.zeros((1, LANES), jnp.int32)
    ends = jnp.zeros((1, LANES), jnp.int32)
    total = jnp.int32(0)
    for d in range(docs):
        size = lens_ref[group, d]
        starts = jnp.where(doc == d, total, starts)
        total = total + size
        ends = jnp.where(doc == d, total, ends)
    positions = first + lax.broadcasted_iota(jnp.int32, (tok, LANES), 0)
    return jnp.where((positions >= starts) & (positions < ends), 1.0, 0.0)


def halves(x):
    high = x.astype(jnp.bfloat16)
    return high, (x - high.astype(jnp.float32)).astype(jnp.bfloat16)


def thirds(x):
    high = x.astype(jnp.bfloat16)
    rest = x - high.astype(jnp.float32)
    return (high,) + halves(rest)


def pool_kernel(
    sizes, lens_hbm, rows_hbm, out_ref, member_ref, scale_ref, inverse_ref, lens_ref, rows_ref, weights_ref, sems
):
    n_dp, _, n_y, n_t = sizes
    docs = lens_ref.shape[1]
    tok, width = rows_ref.shape
    blocks = out_ref.shape[0]
    cut = width // blocks
    lens_copy = pltpu.make_async_copy(lens_hbm, lens_ref, sems.at[CHUNKS])
    lens_copy.start()
    copies = []
    for chunk in range(CHUNKS):
        at = pl.ds(chunk * (tok // CHUNKS), tok // CHUNKS)
        copies.append(pltpu.make_async_copy(rows_hbm.at[at], rows_ref.at[at], sems.at[chunk]))
        copies[-1].start()
    lens_copy.wait()
    shard = (lax.axis_index("z") * n_y + lax.axis_index("y")) * n_t + lax.axis_index("t")
    member_ref[...] = one_hot(lens_ref, lax.axis_index("dp"), shard * tok, docs, tok)
    line = lax.broadcasted_iota(jnp.int32, inverse_ref.shape, 0)
    size = jnp.ones(inverse_ref.shape, jnp.float32)
    for g in range(n_dp):
        for d in range(docs):
            size = jnp.where(line == g * docs + d, lens_ref[g, d].astype(jnp.float32), size)
    inverse_ref[...] = 1.0 / size
    for chunk in range(CHUNKS):
        at = pl.ds(chunk * (tok // CHUNKS), tok // CHUNKS)
        copies[chunk].wait()
        values = rows_ref[at].astype(jnp.float32)
        scale = lax.rsqrt(jnp.sum(values * values, axis=1, keepdims=True) * (1.0 / width) + norm_eps)
        scale_ref[at] = jnp.broadcast_to(scale, (tok // CHUNKS, LANES))
        weights_ref[at] = member_ref[at] * scale
    high, low = halves(jnp.transpose(weights_ref[...])[:DOC_ROWS])
    weights = jnp.concatenate([high, low], axis=0)
    for block in range(blocks):
        part = jnp.dot(
            weights, rows_ref[:, block * cut : (block + 1) * cut], preferred_element_type=jnp.float32
        )
        both = part[:docs] + part[DOC_ROWS : DOC_ROWS + docs]
        for column in range(cut // LANES):
            out_ref[block, column * docs : (column + 1) * docs, :] = both[
                :, column * LANES : (column + 1) * LANES
            ]


def sum_kernel(parts_ref, out_ref):
    total = parts_ref[0]
    for k in range(1, parts_ref.shape[0]):
        total = total + parts_ref[k]
    for k in range(out_ref.shape[0]):
        out_ref[k] = total


def contrast(parts, positive_ref, inverse, group, docs):
    count = parts.shape[0] // 3
    cross = lax.dot_general(parts, parts, (((1,), (1,)), ((), ())), preferred_element_type=jnp.float32)
    cross = cross[:count] + cross[count : 2 * count] + cross[2 * count :]
    gram = cross[:, :count] + cross[:, count : 2 * count] + cross[:, 2 * count :]
    row = lax.broadcasted_iota(jnp.int32, (count, count), 0)
    col = lax.broadcasted_iota(jnp.int32, (count, count), 1)
    diagonal = jnp.where(row == col, gram, 0.0)
    inv_col = 1.0 / jnp.sqrt(jnp.sum(diagonal, axis=1, keepdims=True) + embed_eps)
    inv_row = 1.0 / jnp.sqrt(jnp.sum(diagonal, axis=0, keepdims=True) + embed_eps)
    pair = inv_col * inv_row * (1.0 / tau_value)
    scores = gram * pair
    weights = jnp.where(row == col, 0.0, jnp.exp(scores))
    totals_col = jnp.sum(weights, axis=1, keepdims=True)
    totals_row = jnp.sum(weights, axis=0, keepdims=True)
    picked = jnp.where(positive_ref[...] == row, 1.0, 0.0)
    loss = jnp.sum(
        jnp.log(totals_row) - jnp.sum(scores * picked, axis=0, keepdims=True), axis=1, keepdims=True
    )
    both = weights * (1.0 / totals_col + 1.0 / totals_row) - 2.0 * picked
    along = jnp.sum(both * scores, axis=1, keepdims=True)
    mix = both * pair - jnp.where(row == col, inv_col * inv_col * along, 0.0)
    mix = mix * (loss_factor * inverse[:, :1])
    doc = lax.broadcasted_iota(jnp.int32, (DOC_ROWS, count), 0)
    other = lax.broadcasted_iota(jnp.int32, (DOC_ROWS, count), 1)
    own = jnp.where((other == doc + group * docs) & (doc < docs), 1.0, 0.0)
    return loss, jnp.dot(own, mix, precision=HIGHEST, preferred_element_type=jnp.float32)


def grad_kernel(
    sizes, positive_ref, gain_ref, sums_ref, rows_ref, member_ref, scale_ref, inverse_ref,
    out_hbm, loss_ref, means_ref, parts_ref, grads_ref, weights_ref, out_ref, sems,
):
    n_dp, _, n_y, n_t = sizes
    tok, width = rows_ref.shape
    count = inverse_ref.shape[0]
    docs = count // n_dp
    columns = width // (n_y * n_t) // LANES
    for t in range(n_t):
        for g in range(n_dp):
            for y in range(n_y):
                for column in range(columns):
                    start = ((y * n_t + t) * columns + column) * LANES
                    means_ref[g * docs : (g + 1) * docs, start : start + LANES] = sums_ref[
                        t, g * n_y + y, column * docs : (column + 1) * docs, :
                    ]
    inverse = inverse_ref[...]
    means = means_ref[...] * gain_ref[...] * inverse[:, :1]
    for k, part in enumerate(thirds(means)):
        parts_ref[k * count : (k + 1) * count] = part
    loss, mix = contrast(parts_ref[...], positive_ref, inverse, lax.axis_index("dp"), docs)
    loss_ref[...] = loss
    mix = jnp.concatenate(thirds(jnp.concatenate([mix, mix, mix], axis=1)), axis=0)
    grads = jnp.dot(mix, parts_ref[...], preferred_element_type=jnp.float32)
    grads = grads[:DOC_ROWS] + grads[DOC_ROWS : 2 * DOC_ROWS] + grads[2 * DOC_ROWS :]
    high, low = halves(grads * gain_ref[...])
    grads_ref[:DOC_ROWS] = high
    grads_ref[DOC_ROWS : 2 * DOC_ROWS] = low
    grads_ref[2 * DOC_ROWS :] = high

    member, scale = member_ref[...], scale_ref[...]
    inner = lax.dot_general(
        rows_ref[...], grads_ref[: 2 * DOC_ROWS], (((1,), (1,)), ((), ())), preferred_element_type=jnp.float32
    )
    inner = jnp.sum(inner * member[:, : 2 * DOC_ROWS], axis=1, keepdims=True)
    back = scale[:, :1] * scale[:, :1] * scale[:, :1] * inner * (1.0 / width)
    high, low = halves(member * scale)
    lane = lax.broadcasted_iota(jnp.int32, member.shape, 1)
    weights = jnp.where(lane < 2 * DOC_ROWS, high.astype(jnp.float32), low.astype(jnp.float32))
    weights_ref[...] = weights.astype(jnp.bfloat16)
    copies = []
    for step in range(STEPS):
        at = slice(step * (tok // STEPS), (step + 1) * (tok // STEPS))
        forward = jnp.dot(weights_ref[at, : 3 * DOC_ROWS], grads_ref[...], preferred_element_type=jnp.float32)
        out = forward - rows_ref[at].astype(jnp.float32) * back[at]
        out_ref[at] = out.astype(jnp.bfloat16)
        place = pl.ds(step * (tok // STEPS), tok // STEPS)
        copies.append(pltpu.make_async_copy(out_ref.at[place], out_hbm.at[place], sems.at[step]))
        copies[-1].start()
    for copy in copies:
        copy.wait()


def shards(sizes, hidden, lengths, positive, gain):
    n_dp, n_z, n_y, n_t = sizes
    rows = hidden[0]
    tok, width = rows.shape
    docs = lengths.shape[1]
    count = n_dp * docs
    blocks = n_y * n_t
    lines = docs * width // blocks // LANES
    hbm = pl.BlockSpec(memory_space=pltpu.HBM)
    vmem = pl.BlockSpec(memory_space=pltpu.VMEM)
    params = pltpu.CompilerParams(vmem_limit_bytes=40 * 2**20)

    def array(*dims, dtype=jnp.float32):
        return jax.ShapeDtypeStruct(dims, dtype)

    def summed(parts, copies):
        return pl.pallas_call(
            sum_kernel,
            out_shape=array(copies, lines, LANES),
            in_specs=[vmem],
            out_specs=vmem,
            compiler_params=params,
        )(parts)

    share, member, scale, inverse = pl.pallas_call(
        functools.partial(pool_kernel, sizes),
        out_shape=(array(blocks, lines, LANES), array(tok, LANES), array(tok, LANES), array(count, LANES)),
        in_specs=[hbm, hbm],
        out_specs=(vmem,) * 4,
        scratch_shapes=[
            pltpu.SMEM((n_dp, docs), jnp.int32),
            pltpu.VMEM((tok, width), jnp.bfloat16),
            pltpu.VMEM((tok, LANES), jnp.float32),
            pltpu.SemaphoreType.DMA((CHUNKS + 1,)),
        ],
        compiler_params=params,
    )(pltpu.with_memory_space_constraint(lengths, pltpu.HBM), pltpu.with_memory_space_constraint(rows, pltpu.HBM))
    parts = lax.all_to_all(share, ("y", "t"), 0, 0, tiled=True)
    parts = lax.all_to_all(summed(parts, n_z), "z", 0, 0, tiled=True, axis_index_groups=[list(Z_ORDER)])
    parts = lax.all_to_all(summed(parts, n_dp * n_y), ("dp", "y"), 0, 0, tiled=True)
    sums = lax.all_gather(parts, "t", axis=0)

    grads, loss = pl.pallas_call(
        functools.partial(grad_kernel, sizes),
        out_shape=(array(tok, width, dtype=jnp.bfloat16), array(1, 1)),
        in_specs=[vmem] * 7,
        out_specs=(hbm, vmem),
        scratch_shapes=[
            pltpu.VMEM((count, width), jnp.float32),
            pltpu.VMEM((3 * count, width), jnp.bfloat16),
            pltpu.VMEM((3 * DOC_ROWS, width), jnp.bfloat16),
            pltpu.VMEM((tok, LANES), jnp.bfloat16),
            pltpu.VMEM((tok, width), jnp.bfloat16),
            pltpu.SemaphoreType.DMA((STEPS,)),
        ],
        compiler_params=params,
    )(positive.reshape(1, -1), gain.reshape(1, -1), sums, rows, member, scale, inverse)
    return grads[None], loss.reshape(())


def solution(mesh):
    n_dp, n_seq, n_t = mesh.devices.shape
    n_y = 8 if n_seq % 8 == 0 else 2
    sizes = (n_dp, n_seq // n_y, n_y, n_t)
    inner = Mesh(mesh.devices.reshape(sizes), ("dp", "z", "y", "t"))
    split = P("dp", ("z", "y", "t"), None)
    return jax.shard_map(
        functools.partial(shards, sizes),
        mesh=inner,
        in_specs=(split, P(), P(), P()),
        out_specs=(split, P()),
        check_vma=False,
    )
```

```python
import functools

import jax
import jax.numpy as jnp
from jax import lax
from jax.experimental import pallas as pl
from jax.experimental.pallas import tpu as pltpu
from jax.sharding import Mesh
from jax.sharding import PartitionSpec as P

tau_value = 0.05
loss_factor = 65536.0
norm_eps = 1e-06
embed_eps = 1e-12

LANES = 128
DOC_ROWS = 16
WINDOW = 4
CHUNKS = 4
STEPS = 8
MEANS_ORDER = (24, 16, 8, 0, 28, 20, 12, 4, 25, 17, 9, 1, 29, 21, 13, 5, 26, 18, 10, 2, 30, 22, 14, 6, 27, 19, 11, 3, 31, 23, 15, 7)
Z_ORDER = (11, 5, 10, 4, 9, 3, 8, 2, 7, 1, 6, 0)
HIGHEST = lax.Precision.HIGHEST


def first_doc(lens_ref, group, positions):
    docs = lens_ref.shape[1]
    first = jnp.zeros_like(positions)
    end = jnp.int32(0)
    for d in range(docs):
        end = end + lens_ref[group, d]
        first = first + jnp.where(positions >= end, 1, 0)
    return first


def rounds_needed(lens_ref, tok):
    groups, docs = lens_ref.shape
    rounds = jnp.int32(1)
    for more in range(WINDOW, docs, WINDOW):
        found = jnp.int32(0)
        for g in range(groups):
            starts = [jnp.int32(0)]
            for d in range(docs):
                starts.append(starts[-1] + lens_ref[g, d])
            for d in range(docs - more):
                shared = lax.div(starts[d + more], tok) <= lax.div(starts[d + 1] - 1, tok)
                found = jnp.where(shared, 1, found)
        rounds = rounds + found
    return rounds


def one_hot(lens_ref, group, first, docs, tok):
    lane = lax.broadcasted_iota(jnp.int32, (1, LANES), 1)
    at_first = first_doc(lens_ref, group, jnp.full((1, LANES), first, jnp.int32))
    doc = lane % DOC_ROWS + jnp.where(lane >= LANES // 2, at_first, 0)
    starts = jnp.zeros((1, LANES), jnp.int32)
    ends = jnp.zeros((1, LANES), jnp.int32)
    total = jnp.int32(0)
    for d in range(docs):
        size = lens_ref[group, d]
        starts = jnp.where(doc == d, total, starts)
        total = total + size
        ends = jnp.where(doc == d, total, ends)
    positions = first + lax.broadcasted_iota(jnp.int32, (tok, LANES), 0)
    return jnp.where((positions >= starts) & (positions < ends), 1.0, 0.0)


def halves(x):
    high = x.astype(jnp.bfloat16)
    return high, (x - high.astype(jnp.float32)).astype(jnp.bfloat16)


def thirds(x):
    high = x.astype(jnp.bfloat16)
    rest = x - high.astype(jnp.float32)
    return (high,) + halves(rest)


def pool_kernel(
    sizes, lens_hbm, rows_hbm, out_ref, more_ref, first_ref, rounds_ref, member_ref, scale_ref, inverse_ref,
    rows_ref, lens_ref, weights_ref, sems,
):
    n_dp, _, n_y, n_t = sizes
    docs = lens_ref.shape[1]
    tok, width = rows_ref.shape
    blocks, part_rows, _ = out_ref.shape
    cut = width // blocks
    lens_copy = pltpu.make_async_copy(lens_hbm, lens_ref, sems.at[CHUNKS])
    lens_copy.start()
    copies = []
    for chunk in range(CHUNKS):
        at = pl.ds(chunk * (tok // CHUNKS), tok // CHUNKS)
        copies.append(pltpu.make_async_copy(rows_hbm.at[at], rows_ref.at[at], sems.at[chunk]))
        copies[-1].start()
    lens_copy.wait()
    group, plane = lax.axis_index("dp"), lax.axis_index("z") * (n_y * n_t)
    shard = plane + lax.axis_index("y") * n_t + lax.axis_index("t")
    member_ref[...] = one_hot(lens_ref, group, shard * tok, docs, tok)
    sender = lax.broadcasted_iota(jnp.int32, first_ref.shape, 1) // part_rows
    first_ref[...] = first_doc(lens_ref, group, (plane + sender) * tok)
    rounds_ref[0, 0] = rounds_needed(lens_ref, tok)
    line = lax.broadcasted_iota(jnp.int32, inverse_ref.shape, 0)
    size = jnp.ones(inverse_ref.shape, jnp.float32)
    for g in range(n_dp):
        for d in range(docs):
            size = jnp.where(line == g * docs + d, lens_ref[g, d].astype(jnp.float32), size)
    inverse_ref[...] = 1.0 / size
    for chunk in range(CHUNKS):
        at = pl.ds(chunk * (tok // CHUNKS), tok // CHUNKS)
        copies[chunk].wait()
        values = rows_ref[at].astype(jnp.float32)
        scale = lax.rsqrt(jnp.sum(values * values, axis=1, keepdims=True) * (1.0 / width) + norm_eps)
        scale_ref[at] = jnp.broadcast_to(scale, (tok // CHUNKS, LANES))
        weights_ref[at] = member_ref[at] * scale
    half = LANES // 2
    high, low = halves(jnp.transpose(weights_ref[...])[half : half + DOC_ROWS])
    weights = jnp.concatenate([high, low], axis=0)
    for block in range(blocks):
        part = jnp.dot(
            weights, rows_ref[:, block * cut : (block + 1) * cut], preferred_element_type=jnp.float32
        )
        both = part[:DOC_ROWS] + part[DOC_ROWS:]
        for column in range(cut // LANES):
            at, lanes = slice(column * WINDOW, (column + 1) * WINDOW), slice(column * LANES, (column + 1) * LANES)
            out_ref[block, at] = both[:WINDOW, lanes]
            for r in range(more_ref.shape[0]):
                more_ref[r, block, at] = both[(r + 1) * WINDOW : (r + 2) * WINDOW, lanes]


def place_kernel(docs, round_ref, first_ref, parts_ref, total_ref, out_ref):
    senders, part_rows, _ = parts_ref.shape
    shape = (out_ref.shape[0], senders * part_rows)
    line = lax.broadcasted_iota(jnp.int32, shape, 0)
    lane = lax.broadcasted_iota(jnp.int32, shape, 1) % part_rows
    doc = first_ref[:1, : shape[1]] + lane % WINDOW + round_ref[0, 0] * WINDOW
    here = (line // docs == lane // WINDOW) & (line % docs == doc)
    parts = parts_ref[...].reshape(shape[1], LANES)
    out_ref[...] = total_ref[...] + jnp.dot(
        jnp.where(here, 1.0, 0.0), parts, precision=HIGHEST, preferred_element_type=jnp.float32
    )


def copy_kernel(total_ref, out_ref):
    for k in range(out_ref.shape[0]):
        out_ref[k] = total_ref[...]


def sum_kernel(parts_ref, out_ref):
    total = parts_ref[0]
    for k in range(1, parts_ref.shape[0]):
        total = total + parts_ref[k]
    for k in range(out_ref.shape[0]):
        out_ref[k] = total


def contrast(parts, positive_ref, inverse, group, docs):
    count = parts.shape[0] // 3
    cross = lax.dot_general(parts, parts, (((1,), (1,)), ((), ())), preferred_element_type=jnp.float32)
    cross = cross[:count] + cross[count : 2 * count] + cross[2 * count :]
    gram = cross[:, :count] + cross[:, count : 2 * count] + cross[:, 2 * count :]
    row = lax.broadcasted_iota(jnp.int32, (count, count), 0)
    col = lax.broadcasted_iota(jnp.int32, (count, count), 1)
    diagonal = jnp.where(row == col, gram, 0.0)
    inv_col = 1.0 / jnp.sqrt(jnp.sum(diagonal, axis=1, keepdims=True) + embed_eps)
    inv_row = 1.0 / jnp.sqrt(jnp.sum(diagonal, axis=0, keepdims=True) + embed_eps)
    pair = inv_col * inv_row * (1.0 / tau_value)
    scores = gram * pair
    weights = jnp.where(row == col, 0.0, jnp.exp(scores))
    totals_col = jnp.sum(weights, axis=1, keepdims=True)
    totals_row = jnp.sum(weights, axis=0, keepdims=True)
    picked = jnp.where(positive_ref[...] == row, 1.0, 0.0)
    loss = jnp.sum(
        jnp.log(totals_row) - jnp.sum(scores * picked, axis=0, keepdims=True), axis=1, keepdims=True
    )
    both = weights * (1.0 / totals_col + 1.0 / totals_row) - 2.0 * picked
    along = jnp.sum(both * scores, axis=1, keepdims=True)
    mix = both * pair - jnp.where(row == col, inv_col * inv_col * along, 0.0)
    mix = mix * (loss_factor * inverse[:, :1])
    doc = lax.broadcasted_iota(jnp.int32, (DOC_ROWS, count), 0)
    other = lax.broadcasted_iota(jnp.int32, (DOC_ROWS, count), 1)
    own = jnp.where((other == doc + group * docs) & (doc < docs), 1.0, 0.0)
    return loss, jnp.dot(own, mix, precision=HIGHEST, preferred_element_type=jnp.float32)


def grad_kernel(
    sizes, positive_ref, gain_ref, sums_ref, rows_ref, member_ref, scale_ref, inverse_ref,
    out_hbm, loss_ref, means_ref, parts_ref, grads_ref, out_ref, sems,
):
    n_dp, _, n_y, n_t = sizes
    tok, width = rows_ref.shape
    count = inverse_ref.shape[0]
    docs = count // n_dp
    columns = width // (n_y * n_t) // LANES
    for t in range(n_t):
        for g in range(n_dp):
            for y in range(n_y):
                for column in range(columns):
                    start = ((y * n_t + t) * columns + column) * LANES
                    means_ref[g * docs : (g + 1) * docs, start : start + LANES] = sums_ref[
                        t, MEANS_ORDER.index(g * n_y + y), column * docs : (column + 1) * docs, :
                    ]
    inverse = inverse_ref[...]
    means = means_ref[...] * gain_ref[...] * inverse[:, :1]
    for k, part in enumerate(thirds(means)):
        parts_ref[k * count : (k + 1) * count] = part
    loss, mix = contrast(parts_ref[...], positive_ref, inverse, lax.axis_index("dp"), docs)
    loss_ref[...] = loss
    mix = jnp.concatenate(thirds(jnp.concatenate([mix, mix, mix], axis=1)), axis=0)
    grads = jnp.dot(mix, parts_ref[...], preferred_element_type=jnp.float32)
    grads = grads[:DOC_ROWS] + grads[DOC_ROWS : 2 * DOC_ROWS] + grads[2 * DOC_ROWS :]
    high, low = halves(grads * gain_ref[...])
    grads_ref[:DOC_ROWS] = high
    grads_ref[DOC_ROWS : 2 * DOC_ROWS] = low
    grads_ref[2 * DOC_ROWS :] = high

    copies = []
    for step in range(STEPS):
        at = slice(step * (tok // STEPS), (step + 1) * (tok // STEPS))
        member, scale, rows = member_ref[at], scale_ref[at], rows_ref[at]
        high, low = halves(member * scale)
        lane = lax.broadcasted_iota(jnp.int32, member.shape, 1)
        weights = jnp.where(lane < 2 * DOC_ROWS, high.astype(jnp.float32), low.astype(jnp.float32))
        forward = jnp.dot(
            weights[:, : 3 * DOC_ROWS].astype(jnp.bfloat16), grads_ref[...], preferred_element_type=jnp.float32
        )
        values = rows.astype(jnp.float32)
        inner = jnp.sum(forward * values, axis=1, keepdims=True)
        back = scale[:, :1] * scale[:, :1] * inner * (1.0 / width)
        out_ref[at] = (forward - rows.astype(jnp.float32) * back).astype(jnp.bfloat16)
        place = pl.ds(step * (tok // STEPS), tok // STEPS)
        copies.append(pltpu.make_async_copy(out_ref.at[place], out_hbm.at[place], sems.at[step]))
        copies[-1].start()
    for copy in copies:
        copy.wait()


def shards(sizes, hidden, lengths, positive, gain):
    n_dp, n_z, n_y, n_t = sizes
    rows = hidden[0]
    tok, width = rows.shape
    docs = lengths.shape[1]
    count = n_dp * docs
    blocks = n_y * n_t
    lines = docs * width // blocks // LANES
    hbm = pl.BlockSpec(memory_space=pltpu.HBM)
    vmem = pl.BlockSpec(memory_space=pltpu.VMEM)
    smem = pl.BlockSpec(memory_space=pltpu.SMEM)
    params = pltpu.CompilerParams(vmem_limit_bytes=40 * 2**20)

    def array(*dims, dtype=jnp.float32):
        return jax.ShapeDtypeStruct(dims, dtype)

    def summed(parts, copies):
        return pl.pallas_call(
            sum_kernel,
            out_shape=array(copies, lines, LANES),
            in_specs=[vmem],
            out_specs=vmem,
            compiler_params=params,
        )(parts)

    def placed(r, first, parts, total):
        return pl.pallas_call(
            functools.partial(place_kernel, docs),
            out_shape=array(lines, LANES),
            in_specs=[smem, vmem, vmem, vmem],
            out_specs=vmem,
            compiler_params=params,
        )(jnp.full((1, 1), r, jnp.int32), first, parts, total)

    share, more, first, rounds, member, scale, inverse, held = pl.pallas_call(
        functools.partial(pool_kernel, sizes),
        out_shape=(
            array(blocks, lines // docs * WINDOW, LANES),
            array(-(-docs // WINDOW) - 1, blocks, lines // docs * WINDOW, LANES),
            array(8, LANES, dtype=jnp.int32),
            array(1, 1, dtype=jnp.int32),
            array(tok, LANES),
            array(tok, LANES),
            array(count, LANES),
            array(tok, width, dtype=jnp.bfloat16),
        ),
        in_specs=[hbm, hbm],
        out_specs=(vmem, vmem, vmem, smem, vmem, vmem, vmem, vmem),
        scratch_shapes=[
            pltpu.SMEM((n_dp, docs), jnp.int32),
            pltpu.VMEM((tok, LANES), jnp.float32),
            pltpu.SemaphoreType.DMA((CHUNKS + 1,)),
        ],
        compiler_params=params,
    )(pltpu.with_memory_space_constraint(lengths, pltpu.HBM), pltpu.with_memory_space_constraint(rows, pltpu.HBM))

    def exchange(state):
        r, total = state
        parts = lax.all_to_all(
            lax.dynamic_index_in_dim(more, r - 1, 0, keepdims=False), ("y", "t"), 0, 0, tiled=True
        )
        return r + 1, placed(r, first, parts, total)

    parts = lax.all_to_all(share, ("y", "t"), 0, 0, tiled=True)
    total = placed(0, first, parts, jnp.zeros((lines, LANES), jnp.float32))
    _, total = lax.while_loop(lambda state: state[0] < rounds[0, 0], exchange, (jnp.int32(1), total))
    copies = pl.pallas_call(
        copy_kernel,
        out_shape=array(n_z, lines, LANES),
        in_specs=[vmem],
        out_specs=vmem,
        compiler_params=params,
    )(total)
    parts = lax.all_to_all(copies, "z", 0, 0, tiled=True, axis_index_groups=[list(Z_ORDER)])
    parts = lax.all_to_all(summed(parts, n_dp * n_y), ("dp", "y"), 0, 0, tiled=True, axis_index_groups=[list(MEANS_ORDER)])
    sums = lax.all_gather(parts, "t", axis=0)

    grads, loss = pl.pallas_call(
        functools.partial(grad_kernel, sizes),
        out_shape=(array(tok, width, dtype=jnp.bfloat16), array(1, 1)),
        in_specs=[vmem] * 7,
        out_specs=(hbm, vmem),
        scratch_shapes=[
            pltpu.VMEM((count, width), jnp.float32),
            pltpu.VMEM((3 * count, width), jnp.bfloat16),
            pltpu.VMEM((3 * DOC_ROWS, width), jnp.bfloat16),
            pltpu.VMEM((tok, width), jnp.bfloat16),
            pltpu.SemaphoreType.DMA((STEPS,)),
        ],
        compiler_params=params,
    )(positive.reshape(1, -1), gain.reshape(1, -1), sums, held, member, scale, inverse)
    return grads[None], loss.reshape(())


def solution(mesh):
    n_dp, n_seq, n_t = mesh.devices.shape
    n_y = 8 if n_seq % 8 == 0 else 2
    sizes = (n_dp, n_seq // n_y, n_y, n_t)
    inner = Mesh(mesh.devices.reshape(sizes), ("dp", "z", "y", "t"))
    split = P("dp", ("z", "y", "t"), None)
    return jax.shard_map(
        functools.partial(shards, sizes),
        mesh=inner,
        in_specs=(split, P(), P(), P()),
        out_specs=(split, P()),
        check_vma=False,
    )
```

```python
import functools

import jax
import jax.numpy as jnp
from jax import lax
from jax.experimental import pallas as pl
from jax.experimental.pallas import tpu as pltpu
from jax.sharding import Mesh
from jax.sharding import PartitionSpec as P

tau_value = 0.05
loss_factor = 65536.0
norm_eps = 1e-06
embed_eps = 1e-12

LANES = 128
DOC_ROWS = 16
WINDOW = 4
CHUNKS = 4
STEPS = 8
MEANS_ORDER = (24, 16, 8, 0, 28, 20, 12, 4, 25, 17, 9, 1, 29, 21, 13, 5, 26, 18, 10, 2, 30, 22, 14, 6, 27, 19, 11, 3, 31, 23, 15, 7)
Z_ORDER = (11, 5, 10, 4, 9, 3, 8, 2, 7, 1, 6, 0)
HIGHEST = lax.Precision.HIGHEST


def first_doc(lens_ref, group, positions):
    docs = lens_ref.shape[1]
    first = jnp.zeros_like(positions)
    end = jnp.int32(0)
    for d in range(docs):
        end = end + lens_ref[group, d]
        first = first + jnp.where(positions >= end, 1, 0)
    return first


def rounds_needed(lens_ref, tok):
    groups, docs = lens_ref.shape
    rounds = jnp.int32(1)
    for more in range(WINDOW, docs, WINDOW):
        found = jnp.int32(0)
        for g in range(groups):
            starts = [jnp.int32(0)]
            for d in range(docs):
                starts.append(starts[-1] + lens_ref[g, d])
            for d in range(docs - more):
                shared = lax.div(starts[d + more], tok) <= lax.div(starts[d + 1] - 1, tok)
                found = jnp.where(shared, 1, found)
        rounds = rounds + found
    return rounds


def one_hot(lens_ref, group, first, docs, tok):
    lane = lax.broadcasted_iota(jnp.int32, (1, LANES), 1)
    at_first = first_doc(lens_ref, group, jnp.full((1, LANES), first, jnp.int32))
    doc = lane % DOC_ROWS + jnp.where(lane >= LANES // 2, at_first, 0)
    starts = jnp.zeros((1, LANES), jnp.int32)
    ends = jnp.zeros((1, LANES), jnp.int32)
    total = jnp.int32(0)
    for d in range(docs):
        size = lens_ref[group, d]
        starts = jnp.where(doc == d, total, starts)
        total = total + size
        ends = jnp.where(doc == d, total, ends)
    positions = first + lax.broadcasted_iota(jnp.int32, (tok, LANES), 0)
    return jnp.where((positions >= starts) & (positions < ends), 1.0, 0.0)


def halves(x):
    high = x.astype(jnp.bfloat16)
    return high, (x - high.astype(jnp.float32)).astype(jnp.bfloat16)


def thirds(x):
    high = x.astype(jnp.bfloat16)
    rest = x - high.astype(jnp.float32)
    return (high,) + halves(rest)


def pool_kernel(
    sizes, lens_hbm, rows_hbm, out_ref, more_ref, first_ref, rounds_ref, member_ref, scale_ref, inverse_ref,
    rows_ref, lens_ref, weights_ref, sems,
):
    n_dp, _, n_y, n_t = sizes
    docs = lens_ref.shape[1]
    tok, width = rows_ref.shape
    blocks, part_rows, _ = out_ref.shape
    cut = width // blocks
    lens_copy = pltpu.make_async_copy(lens_hbm, lens_ref, sems.at[CHUNKS])
    lens_copy.start()
    copies = []
    for chunk in range(CHUNKS):
        at = pl.ds(chunk * (tok // CHUNKS), tok // CHUNKS)
        copies.append(pltpu.make_async_copy(rows_hbm.at[at], rows_ref.at[at], sems.at[chunk]))
        copies[-1].start()
    lens_copy.wait()
    group, plane = lax.axis_index("dp"), lax.axis_index("z") * (n_y * n_t)
    shard = plane + lax.axis_index("y") * n_t + lax.axis_index("t")
    member_ref[...] = one_hot(lens_ref, group, shard * tok, docs, tok)
    sender = lax.broadcasted_iota(jnp.int32, first_ref.shape, 1) // part_rows
    first_ref[...] = first_doc(lens_ref, group, (plane + sender) * tok)
    rounds_ref[0, 0] = rounds_needed(lens_ref, tok)
    line = lax.broadcasted_iota(jnp.int32, inverse_ref.shape, 0)
    size = jnp.ones(inverse_ref.shape, jnp.float32)
    for g in range(n_dp):
        for d in range(docs):
            size = jnp.where(line == g * docs + d, lens_ref[g, d].astype(jnp.float32), size)
    inverse_ref[...] = 1.0 / size
    for chunk in range(CHUNKS):
        at = pl.ds(chunk * (tok // CHUNKS), tok // CHUNKS)
        copies[chunk].wait()
        values = rows_ref[at].astype(jnp.float32)
        scale = lax.rsqrt(jnp.sum(values * values, axis=1, keepdims=True) * (1.0 / width) + norm_eps)
        scale_ref[at] = jnp.broadcast_to(scale, (tok // CHUNKS, LANES))
        weights_ref[at] = member_ref[at] * scale
    half = LANES // 2
    high, low = halves(jnp.transpose(weights_ref[...])[half : half + DOC_ROWS])
    weights = jnp.concatenate([high, low], axis=0)
    for block in range(blocks):
        part = jnp.dot(
            weights, rows_ref[:, block * cut : (block + 1) * cut], preferred_element_type=jnp.float32
        )
        both = part[:DOC_ROWS] + part[DOC_ROWS:]
        for column in range(cut // LANES):
            at, lanes = slice(column * WINDOW, (column + 1) * WINDOW), slice(column * LANES, (column + 1) * LANES)
            out_ref[block, at] = both[:WINDOW, lanes]
            for r in range(more_ref.shape[0]):
                more_ref[r, block, at] = both[(r + 1) * WINDOW : (r + 2) * WINDOW, lanes]


def place_kernel(docs, round_ref, first_ref, parts_ref, total_ref, out_ref):
    senders, part_rows, _ = parts_ref.shape
    shape = (out_ref.shape[1], senders * part_rows)
    line = lax.broadcasted_iota(jnp.int32, shape, 0)
    lane = lax.broadcasted_iota(jnp.int32, shape, 1) % part_rows
    doc = first_ref[:1, : shape[1]] + lane % WINDOW + round_ref[0, 0] * WINDOW
    here = (line // docs == lane // WINDOW) & (line % docs == doc)
    parts = parts_ref[...].reshape(shape[1], LANES)
    total = total_ref[...] + jnp.dot(
        jnp.where(here, 1.0, 0.0), parts, precision=HIGHEST, preferred_element_type=jnp.float32
    )
    for k in range(out_ref.shape[0]):
        out_ref[k] = total


def sum_kernel(parts_ref, out_ref):
    total = parts_ref[0]
    for k in range(1, parts_ref.shape[0]):
        total = total + parts_ref[k]
    for k in range(out_ref.shape[0]):
        out_ref[k] = total


def contrast(parts, positive_ref, inverse, group, docs):
    count = parts.shape[0] // 3
    cross = lax.dot_general(parts, parts, (((1,), (1,)), ((), ())), preferred_element_type=jnp.float32)
    cross = cross[:count] + cross[count : 2 * count] + cross[2 * count :]
    gram = cross[:, :count] + cross[:, count : 2 * count] + cross[:, 2 * count :]
    row = lax.broadcasted_iota(jnp.int32, (count, count), 0)
    col = lax.broadcasted_iota(jnp.int32, (count, count), 1)
    diagonal = jnp.where(row == col, gram, 0.0)
    inv_col = 1.0 / jnp.sqrt(jnp.sum(diagonal, axis=1, keepdims=True) + embed_eps)
    inv_row = 1.0 / jnp.sqrt(jnp.sum(diagonal, axis=0, keepdims=True) + embed_eps)
    pair = inv_col * inv_row * (1.0 / tau_value)
    scores = gram * pair
    weights = jnp.where(row == col, 0.0, jnp.exp(scores))
    totals_col = jnp.sum(weights, axis=1, keepdims=True)
    totals_row = jnp.sum(weights, axis=0, keepdims=True)
    picked = jnp.where(positive_ref[...] == row, 1.0, 0.0)
    loss = jnp.sum(
        jnp.log(totals_row) - jnp.sum(scores * picked, axis=0, keepdims=True), axis=1, keepdims=True
    )
    both = weights * (1.0 / totals_col + 1.0 / totals_row) - 2.0 * picked
    along = jnp.sum(both * scores, axis=1, keepdims=True)
    mix = both * pair - jnp.where(row == col, inv_col * inv_col * along, 0.0)
    mix = mix * (loss_factor * inverse[:, :1])
    doc = lax.broadcasted_iota(jnp.int32, (DOC_ROWS, count), 0)
    other = lax.broadcasted_iota(jnp.int32, (DOC_ROWS, count), 1)
    own = jnp.where((other == doc + group * docs) & (doc < docs), 1.0, 0.0)
    return loss, jnp.dot(own, mix, precision=HIGHEST, preferred_element_type=jnp.float32)


def grad_kernel(
    sizes, positive_ref, gain_ref, sums_ref, rows_ref, member_ref, scale_ref, inverse_ref,
    out_hbm, loss_ref, means_ref, parts_ref, grads_ref, out_ref, sems,
):
    n_dp, _, n_y, n_t = sizes
    tok, width = rows_ref.shape
    count = inverse_ref.shape[0]
    docs = count // n_dp
    columns = width // (n_y * n_t) // LANES
    for t in range(n_t):
        for g in range(n_dp):
            for y in range(n_y):
                for column in range(columns):
                    start = ((y * n_t + t) * columns + column) * LANES
                    means_ref[g * docs : (g + 1) * docs, start : start + LANES] = sums_ref[
                        t, MEANS_ORDER.index(g * n_y + y), column * docs : (column + 1) * docs, :
                    ]
    inverse = inverse_ref[...]
    means = means_ref[...] * gain_ref[...] * inverse[:, :1]
    for k, part in enumerate(thirds(means)):
        parts_ref[k * count : (k + 1) * count] = part
    loss, mix = contrast(parts_ref[...], positive_ref, inverse, lax.axis_index("dp"), docs)
    loss_ref[...] = loss
    mix = jnp.concatenate(thirds(jnp.concatenate([mix, mix, mix], axis=1)), axis=0)
    grads = jnp.dot(mix, parts_ref[...], preferred_element_type=jnp.float32)
    grads = grads[:DOC_ROWS] + grads[DOC_ROWS : 2 * DOC_ROWS] + grads[2 * DOC_ROWS :]
    high, low = halves(grads * gain_ref[...])
    grads_ref[:DOC_ROWS] = high
    grads_ref[DOC_ROWS : 2 * DOC_ROWS] = low
    grads_ref[2 * DOC_ROWS :] = high

    copies = []
    for step in range(STEPS):
        at = slice(step * (tok // STEPS), (step + 1) * (tok // STEPS))
        member, scale, rows = member_ref[at], scale_ref[at], rows_ref[at]
        high, low = halves(member * scale)
        lane = lax.broadcasted_iota(jnp.int32, member.shape, 1)
        weights = jnp.where(lane < 2 * DOC_ROWS, high.astype(jnp.float32), low.astype(jnp.float32))
        forward = jnp.dot(
            weights[:, : 3 * DOC_ROWS].astype(jnp.bfloat16), grads_ref[...], preferred_element_type=jnp.float32
        )
        values = rows.astype(jnp.float32)
        inner = jnp.sum(forward * values, axis=1, keepdims=True)
        back = scale[:, :1] * scale[:, :1] * inner * (1.0 / width)
        out_ref[at] = (forward - rows.astype(jnp.float32) * back).astype(jnp.bfloat16)
        place = pl.ds(step * (tok // STEPS), tok // STEPS)
        copies.append(pltpu.make_async_copy(out_ref.at[place], out_hbm.at[place], sems.at[step]))
        copies[-1].start()
    for copy in copies:
        copy.wait()


def shards(sizes, hidden, lengths, positive, gain):
    n_dp, n_z, n_y, n_t = sizes
    rows = hidden[0]
    tok, width = rows.shape
    docs = lengths.shape[1]
    count = n_dp * docs
    blocks = n_y * n_t
    lines = docs * width // blocks // LANES
    hbm = pl.BlockSpec(memory_space=pltpu.HBM)
    vmem = pl.BlockSpec(memory_space=pltpu.VMEM)
    smem = pl.BlockSpec(memory_space=pltpu.SMEM)
    params = pltpu.CompilerParams(vmem_limit_bytes=40 * 2**20)

    def array(*dims, dtype=jnp.float32):
        return jax.ShapeDtypeStruct(dims, dtype)

    def summed(parts, copies):
        return pl.pallas_call(
            sum_kernel,
            out_shape=array(copies, lines, LANES),
            in_specs=[vmem],
            out_specs=vmem,
            compiler_params=params,
        )(parts)

    def placed(r, first, parts, total, copies):
        return pl.pallas_call(
            functools.partial(place_kernel, docs),
            out_shape=array(copies, lines, LANES),
            in_specs=[smem, vmem, vmem, vmem],
            out_specs=vmem,
            compiler_params=params,
        )(jnp.full((1, 1), r, jnp.int32), first, parts, total)

    share, more, first, rounds, member, scale, inverse, held = pl.pallas_call(
        functools.partial(pool_kernel, sizes),
        out_shape=(
            array(blocks, lines // docs * WINDOW, LANES),
            array(-(-docs // WINDOW) - 1, blocks, lines // docs * WINDOW, LANES),
            array(8, LANES, dtype=jnp.int32),
            array(1, 1, dtype=jnp.int32),
            array(tok, LANES),
            array(tok, LANES),
            array(count, LANES),
            array(tok, width, dtype=jnp.bfloat16),
        ),
        in_specs=[hbm, hbm],
        out_specs=(vmem, vmem, vmem, smem, vmem, vmem, vmem, vmem),
        scratch_shapes=[
            pltpu.SMEM((n_dp, docs), jnp.int32),
            pltpu.VMEM((tok, LANES), jnp.float32),
            pltpu.SemaphoreType.DMA((CHUNKS + 1,)),
        ],
        compiler_params=params,
    )(pltpu.with_memory_space_constraint(lengths, pltpu.HBM), pltpu.with_memory_space_constraint(rows, pltpu.HBM))

    def exchange(state):
        r, total = state
        parts = lax.all_to_all(
            lax.dynamic_index_in_dim(more, r - 1, 0, keepdims=False), ("y", "t"), 0, 0, tiled=True
        )
        return r + 1, placed(r, first, parts, total, 1)[0]

    _, rest = lax.while_loop(
        lambda state: state[0] < rounds[0, 0], exchange, (jnp.int32(1), jnp.zeros((lines, LANES), jnp.float32))
    )
    parts = lax.all_to_all(share, ("y", "t"), 0, 0, tiled=True)
    copies = placed(0, first, parts, rest, n_z)
    parts = lax.all_to_all(copies, "z", 0, 0, tiled=True, axis_index_groups=[list(Z_ORDER)])
    parts = lax.all_to_all(summed(parts, n_dp * n_y), ("dp", "y"), 0, 0, tiled=True, axis_index_groups=[list(MEANS_ORDER)])
    sums = lax.all_gather(parts, "t", axis=0)

    grads, loss = pl.pallas_call(
        functools.partial(grad_kernel, sizes),
        out_shape=(array(tok, width, dtype=jnp.bfloat16), array(1, 1)),
        in_specs=[vmem] * 7,
        out_specs=(hbm, vmem),
        scratch_shapes=[
            pltpu.VMEM((count, width), jnp.float32),
            pltpu.VMEM((3 * count, width), jnp.bfloat16),
            pltpu.VMEM((3 * DOC_ROWS, width), jnp.bfloat16),
            pltpu.VMEM((tok, width), jnp.bfloat16),
            pltpu.SemaphoreType.DMA((STEPS,)),
        ],
        compiler_params=params,
    )(positive.reshape(1, -1), gain.reshape(1, -1), sums, held, member, scale, inverse)
    return grads[None], loss.reshape(())


def solution(mesh):
    n_dp, n_seq, n_t = mesh.devices.shape
    n_y = 8 if n_seq % 8 == 0 else 2
    sizes = (n_dp, n_seq // n_y, n_y, n_t)
    inner = Mesh(mesh.devices.reshape(sizes), ("dp", "z", "y", "t"))
    split = P("dp", ("z", "y", "t"), None)
    return jax.shard_map(
        functools.partial(shards, sizes),
        mesh=inner,
        in_specs=(split, P(), P(), P()),
        out_specs=(split, P()),
        check_vma=False,
    )
```

```python
import functools

import jax
import jax.numpy as jnp
from jax import lax
from jax.experimental import pallas as pl
from jax.experimental.pallas import tpu as pltpu
from jax.sharding import Mesh
from jax.sharding import PartitionSpec as P

tau_value = 0.05
loss_factor = 65536.0
norm_eps = 1e-06
embed_eps = 1e-12

LANES = 128
DOC_ROWS = 16
WINDOW = 4
CHUNKS = 4
STEPS = 8
MEANS_ORDER = (24, 16, 8, 0, 28, 20, 12, 4, 25, 17, 9, 1, 29, 21, 13, 5, 26, 18, 10, 2, 30, 22, 14, 6, 27, 19, 11, 3, 31, 23, 15, 7)
Z_ORDER = (11, 5, 10, 4, 9, 3, 8, 2, 7, 1, 6, 0)
HIGHEST = lax.Precision.HIGHEST


def first_doc(lens_ref, group, positions):
    docs = lens_ref.shape[1]
    first = jnp.zeros_like(positions)
    end = jnp.int32(0)
    for d in range(docs):
        end = end + lens_ref[group, d]
        first = first + jnp.where(positions >= end, 1, 0)
    return first


def rounds_needed(lens_ref, tok):
    groups, docs = lens_ref.shape
    rounds = jnp.int32(1)
    for more in range(WINDOW, docs, WINDOW):
        found = jnp.int32(0)
        for g in range(groups):
            starts = [jnp.int32(0)]
            for d in range(docs):
                starts.append(starts[-1] + lens_ref[g, d])
            for d in range(docs - more):
                shared = lax.div(starts[d + more], tok) <= lax.div(starts[d + 1] - 1, tok)
                found = jnp.where(shared, 1, found)
        rounds = rounds + found
    return rounds


def one_hot(lens_ref, group, first, docs, tok):
    lane = lax.broadcasted_iota(jnp.int32, (1, LANES), 1)
    at_first = first_doc(lens_ref, group, jnp.full((1, LANES), first, jnp.int32))
    doc = lane % DOC_ROWS + jnp.where(lane >= LANES // 2, at_first, 0)
    starts = jnp.zeros((1, LANES), jnp.int32)
    ends = jnp.zeros((1, LANES), jnp.int32)
    total = jnp.int32(0)
    for d in range(docs):
        size = lens_ref[group, d]
        starts = jnp.where(doc == d, total, starts)
        total = total + size
        ends = jnp.where(doc == d, total, ends)
    positions = first + lax.broadcasted_iota(jnp.int32, (tok, LANES), 0)
    return jnp.where((positions >= starts) & (positions < ends), 1.0, 0.0)


def halves(x):
    high = x.astype(jnp.bfloat16)
    return high, (x - high.astype(jnp.float32)).astype(jnp.bfloat16)


def thirds(x):
    high = x.astype(jnp.bfloat16)
    rest = x - high.astype(jnp.float32)
    return (high,) + halves(rest)


def pool_kernel(
    sizes, lens_hbm, rows_hbm, out_ref, more_ref, first_ref, rounds_ref, forward_ref, scale_ref, inverse_ref,
    rows_ref, lens_ref, member_ref, weights_ref, sems,
):
    n_dp, _, n_y, n_t = sizes
    docs = lens_ref.shape[1]
    tok, width = rows_ref.shape
    blocks, part_rows, _ = out_ref.shape
    cut = width // blocks
    lens_copy = pltpu.make_async_copy(lens_hbm, lens_ref, sems.at[CHUNKS])
    lens_copy.start()
    copies = []
    for chunk in range(CHUNKS):
        at = pl.ds(chunk * (tok // CHUNKS), tok // CHUNKS)
        copies.append(pltpu.make_async_copy(rows_hbm.at[at], rows_ref.at[at], sems.at[chunk]))
        copies[-1].start()
    lens_copy.wait()
    group, plane = lax.axis_index("dp"), lax.axis_index("z") * (n_y * n_t)
    shard = plane + lax.axis_index("y") * n_t + lax.axis_index("t")
    member_ref[...] = one_hot(lens_ref, group, shard * tok, docs, tok)
    sender = lax.broadcasted_iota(jnp.int32, first_ref.shape, 1) // part_rows
    first_ref[...] = first_doc(lens_ref, group, (plane + sender) * tok)
    rounds_ref[0, 0] = rounds_needed(lens_ref, tok)
    line = lax.broadcasted_iota(jnp.int32, inverse_ref.shape, 0)
    size = jnp.ones(inverse_ref.shape, jnp.float32)
    for g in range(n_dp):
        for d in range(docs):
            size = jnp.where(line == g * docs + d, lens_ref[g, d].astype(jnp.float32), size)
    inverse_ref[...] = 1.0 / size
    for chunk in range(CHUNKS):
        at = pl.ds(chunk * (tok // CHUNKS), tok // CHUNKS)
        copies[chunk].wait()
        values = rows_ref[at].astype(jnp.float32)
        scale = lax.rsqrt(jnp.sum(values * values, axis=1, keepdims=True) * (1.0 / width) + norm_eps)
        scale_ref[at] = jnp.broadcast_to(scale, (tok // CHUNKS, LANES))
        weights = member_ref[at] * scale
        weights_ref[at] = weights
        high, low = halves(weights)
        lane = lax.broadcasted_iota(jnp.int32, weights.shape, 1)
        forward = jnp.where(lane < 2 * DOC_ROWS, high.astype(jnp.float32), low.astype(jnp.float32))
        forward_ref[at] = forward.astype(jnp.bfloat16)
    half = LANES // 2
    high, low = halves(jnp.transpose(weights_ref[...])[half : half + DOC_ROWS])
    weights = jnp.concatenate([high, low], axis=0)
    for block in range(blocks):
        part = jnp.dot(
            weights, rows_ref[:, block * cut : (block + 1) * cut], preferred_element_type=jnp.float32
        )
        both = part[:DOC_ROWS] + part[DOC_ROWS:]
        for column in range(cut // LANES):
            at, lanes = slice(column * WINDOW, (column + 1) * WINDOW), slice(column * LANES, (column + 1) * LANES)
            out_ref[block, at] = both[:WINDOW, lanes]
            for r in range(more_ref.shape[0]):
                more_ref[r, block, at] = both[(r + 1) * WINDOW : (r + 2) * WINDOW, lanes]


def place_kernel(docs, round_ref, first_ref, parts_ref, total_ref, out_ref):
    senders, part_rows, _ = parts_ref.shape
    shape = (out_ref.shape[1], senders * part_rows)
    line = lax.broadcasted_iota(jnp.int32, shape, 0)
    lane = lax.broadcasted_iota(jnp.int32, shape, 1) % part_rows
    doc = first_ref[:1, : shape[1]] + lane % WINDOW + round_ref[0, 0] * WINDOW
    here = (line // docs == lane // WINDOW) & (line % docs == doc)
    parts = parts_ref[...].reshape(shape[1], LANES)
    total = total_ref[...] + jnp.dot(
        jnp.where(here, 1.0, 0.0), parts, precision=HIGHEST, preferred_element_type=jnp.float32
    )
    for k in range(out_ref.shape[0]):
        out_ref[k] = total


def sum_kernel(parts_ref, out_ref):
    total = parts_ref[0]
    for k in range(1, parts_ref.shape[0]):
        total = total + parts_ref[k]
    for k in range(out_ref.shape[0]):
        out_ref[k] = total


def contrast(parts, positive_ref, inverse, group, docs):
    count = parts.shape[0] // 3
    cross = lax.dot_general(parts, parts, (((1,), (1,)), ((), ())), preferred_element_type=jnp.float32)
    cross = cross[:count] + cross[count : 2 * count] + cross[2 * count :]
    gram = cross[:, :count] + cross[:, count : 2 * count] + cross[:, 2 * count :]
    row = lax.broadcasted_iota(jnp.int32, (count, count), 0)
    col = lax.broadcasted_iota(jnp.int32, (count, count), 1)
    diagonal = jnp.where(row == col, gram, 0.0)
    inv_col = 1.0 / jnp.sqrt(jnp.sum(diagonal, axis=1, keepdims=True) + embed_eps)
    inv_row = 1.0 / jnp.sqrt(jnp.sum(diagonal, axis=0, keepdims=True) + embed_eps)
    pair = inv_col * inv_row * (1.0 / tau_value)
    scores = gram * pair
    weights = jnp.where(row == col, 0.0, jnp.exp(scores))
    totals_col = jnp.sum(weights, axis=1, keepdims=True)
    totals_row = jnp.sum(weights, axis=0, keepdims=True)
    picked = jnp.where(positive_ref[...] == row, 1.0, 0.0)
    loss = jnp.sum(
        jnp.log(totals_row) - jnp.sum(scores * picked, axis=0, keepdims=True), axis=1, keepdims=True
    )
    both = weights * (1.0 / totals_col + 1.0 / totals_row) - 2.0 * picked
    along = jnp.sum(both * scores, axis=1, keepdims=True)
    mix = both * pair - jnp.where(row == col, inv_col * inv_col * along, 0.0)
    mix = mix * (loss_factor * inverse[:, :1])
    doc = lax.broadcasted_iota(jnp.int32, (DOC_ROWS, count), 0)
    other = lax.broadcasted_iota(jnp.int32, (DOC_ROWS, count), 1)
    own = jnp.where((other == doc + group * docs) & (doc < docs), 1.0, 0.0)
    return loss, jnp.dot(own, mix, precision=HIGHEST, preferred_element_type=jnp.float32)


def grad_kernel(
    sizes, positive_ref, gain_ref, sums_ref, rows_ref, forward_ref, scale_ref, inverse_ref,
    out_hbm, loss_ref, means_ref, parts_ref, grads_ref, out_ref, sems,
):
    n_dp, _, n_y, n_t = sizes
    tok, width = rows_ref.shape
    count = inverse_ref.shape[0]
    docs = count // n_dp
    columns = width // (n_y * n_t) // LANES
    for t in range(n_t):
        for g in range(n_dp):
            for y in range(n_y):
                for column in range(columns):
                    start = ((y * n_t + t) * columns + column) * LANES
                    means_ref[g * docs : (g + 1) * docs, start : start + LANES] = sums_ref[
                        t, MEANS_ORDER.index(g * n_y + y), column * docs : (column + 1) * docs, :
                    ]
    inverse = inverse_ref[...]
    means = means_ref[...] * gain_ref[...] * inverse[:, :1]
    for k, part in enumerate(thirds(means)):
        parts_ref[k * count : (k + 1) * count] = part
    loss, mix = contrast(parts_ref[...], positive_ref, inverse, lax.axis_index("dp"), docs)
    loss_ref[...] = loss
    mix = jnp.concatenate(thirds(jnp.concatenate([mix, mix, mix], axis=1)), axis=0)
    grads = jnp.dot(mix, parts_ref[...], preferred_element_type=jnp.float32)
    grads = grads[:DOC_ROWS] + grads[DOC_ROWS : 2 * DOC_ROWS] + grads[2 * DOC_ROWS :]
    high, low = halves(grads * gain_ref[...])
    grads_ref[:DOC_ROWS] = high
    grads_ref[DOC_ROWS : 2 * DOC_ROWS] = low
    grads_ref[2 * DOC_ROWS :] = high

    copies = []
    for step in range(STEPS):
        at = slice(step * (tok // STEPS), (step + 1) * (tok // STEPS))
        scale, rows = scale_ref[at], rows_ref[at]
        forward = jnp.dot(
            forward_ref[at, : 3 * DOC_ROWS], grads_ref[...], preferred_element_type=jnp.float32
        )
        values = rows.astype(jnp.float32)
        inner = jnp.sum(forward * values, axis=1, keepdims=True)
        back = scale[:, :1] * scale[:, :1] * inner * (1.0 / width)
        out_ref[at] = (forward - rows.astype(jnp.float32) * back).astype(jnp.bfloat16)
        place = pl.ds(step * (tok // STEPS), tok // STEPS)
        copies.append(pltpu.make_async_copy(out_ref.at[place], out_hbm.at[place], sems.at[step]))
        copies[-1].start()
    for copy in copies:
        copy.wait()


def shards(sizes, hidden, lengths, positive, gain):
    n_dp, n_z, n_y, n_t = sizes
    rows = hidden[0]
    tok, width = rows.shape
    docs = lengths.shape[1]
    count = n_dp * docs
    blocks = n_y * n_t
    lines = docs * width // blocks // LANES
    hbm = pl.BlockSpec(memory_space=pltpu.HBM)
    vmem = pl.BlockSpec(memory_space=pltpu.VMEM)
    smem = pl.BlockSpec(memory_space=pltpu.SMEM)
    params = pltpu.CompilerParams(vmem_limit_bytes=40 * 2**20)

    def array(*dims, dtype=jnp.float32):
        return jax.ShapeDtypeStruct(dims, dtype)

    def summed(parts, copies):
        return pl.pallas_call(
            sum_kernel,
            out_shape=array(copies, lines, LANES),
            in_specs=[vmem],
            out_specs=vmem,
            compiler_params=params,
        )(parts)

    def placed(r, first, parts, total, copies):
        return pl.pallas_call(
            functools.partial(place_kernel, docs),
            out_shape=array(copies, lines, LANES),
            in_specs=[smem, vmem, vmem, vmem],
            out_specs=vmem,
            compiler_params=params,
        )(jnp.full((1, 1), r, jnp.int32), first, parts, total)

    share, more, first, rounds, forward, scale, inverse, held = pl.pallas_call(
        functools.partial(pool_kernel, sizes),
        out_shape=(
            array(blocks, lines // docs * WINDOW, LANES),
            array(-(-docs // WINDOW) - 1, blocks, lines // docs * WINDOW, LANES),
            array(8, LANES, dtype=jnp.int32),
            array(1, 1, dtype=jnp.int32),
            array(tok, LANES, dtype=jnp.bfloat16),
            array(tok, LANES),
            array(count, LANES),
            array(tok, width, dtype=jnp.bfloat16),
        ),
        in_specs=[hbm, hbm],
        out_specs=(vmem, vmem, vmem, smem, vmem, vmem, vmem, vmem),
        scratch_shapes=[
            pltpu.SMEM((n_dp, docs), jnp.int32),
            pltpu.VMEM((tok, LANES), jnp.float32),
            pltpu.VMEM((tok, LANES), jnp.float32),
            pltpu.SemaphoreType.DMA((CHUNKS + 1,)),
        ],
        compiler_params=params,
    )(pltpu.with_memory_space_constraint(lengths, pltpu.HBM), pltpu.with_memory_space_constraint(rows, pltpu.HBM))

    def exchange(state):
        r, total = state
        parts = lax.all_to_all(
            lax.dynamic_index_in_dim(more, r - 1, 0, keepdims=False), ("y", "t"), 0, 0, tiled=True
        )
        return r + 1, placed(r, first, parts, total, 1)[0]

    _, rest = lax.while_loop(
        lambda state: state[0] < rounds[0, 0], exchange, (jnp.int32(1), jnp.zeros((lines, LANES), jnp.float32))
    )
    parts = lax.all_to_all(share, ("y", "t"), 0, 0, tiled=True)
    copies = placed(0, first, parts, rest, n_z)
    parts = lax.all_to_all(copies, "z", 0, 0, tiled=True, axis_index_groups=[list(Z_ORDER)])
    parts = lax.all_to_all(summed(parts, n_dp * n_y), ("dp", "y"), 0, 0, tiled=True, axis_index_groups=[list(MEANS_ORDER)])
    sums = lax.all_gather(parts, "t", axis=0)

    grads, loss = pl.pallas_call(
        functools.partial(grad_kernel, sizes),
        out_shape=(array(tok, width, dtype=jnp.bfloat16), array(1, 1)),
        in_specs=[vmem] * 7,
        out_specs=(hbm, vmem),
        scratch_shapes=[
            pltpu.VMEM((count, width), jnp.float32),
            pltpu.VMEM((3 * count, width), jnp.bfloat16),
            pltpu.VMEM((3 * DOC_ROWS, width), jnp.bfloat16),
            pltpu.VMEM((tok, width), jnp.bfloat16),
            pltpu.SemaphoreType.DMA((STEPS,)),
        ],
        compiler_params=params,
    )(positive.reshape(1, -1), gain.reshape(1, -1), sums, held, forward, scale, inverse)
    return grads[None], loss.reshape(())


def solution(mesh):
    n_dp, n_seq, n_t = mesh.devices.shape
    n_y = 8 if n_seq % 8 == 0 else 2
    sizes = (n_dp, n_seq // n_y, n_y, n_t)
    inner = Mesh(mesh.devices.reshape(sizes), ("dp", "z", "y", "t"))
    split = P("dp", ("z", "y", "t"), None)
    return jax.shard_map(
        functools.partial(shards, sizes),
        mesh=inner,
        in_specs=(split, P(), P(), P()),
        out_specs=(split, P()),
        check_vma=False,
    )
```
